32 devices in a mesh: groups: 2 (over y), expert: 4 (over x, core), tensor: 4 (over z).
Axes of the slice: x: 2, y: 2, z: 4, core: 2. Of those that a mesh axis runs over, the one named last changes fastest.
Arguments:
- tokens: bfloat16 [2048, 2048], P(('groups', 'expert')), parts along dimension 0, may hold values from -6 to 6
- route_ids: int32 [2048, 2], P(('groups', 'expert')), parts along dimension 0, may hold values from 0 to 3, all different within a row; in each aligned block of 256 rows (0 to 255, 256 to 511, ...) at most 256 rows name the same one
- route_weights: float32 [2048, 2], P(('groups', 'expert')), parts along dimension 0, may hold values from 0.2 to 1
- modulation: float32 [8, 6144], P(('groups', 'expert')), parts along dimension 0, may hold values from -5 to 5
- partner: int32 [4], replicated, may hold values from 0 to 3, as said below
- w_gate: bfloat16 [4, 2048, 4096], P('expert', None, 'tensor'), may hold values from -0.125 to 0.125
- w_up: bfloat16 [4, 2048, 4096], P('expert', None, 'tensor'), may hold values from -0.125 to 0.125
- w_down: bfloat16 [4, 4096, 2048], P('expert', 'tensor'), may hold values from -0.09375 to 0.09375
- spare_gate: bfloat16 [4, 2048, 4096], P('expert', None, 'tensor'), may hold values from -0.125 to 0.125
- spare_up: bfloat16 [4, 2048, 4096], P('expert', None, 'tensor'), may hold values from -0.125 to 0.125
- spare_down: bfloat16 [4, 4096, 2048], P('expert', 'tensor'), may hold values from -0.09375 to 0.09375
Outputs:
- layer_out: bfloat16 [2048, 2048], P(('groups', 'expert'), 'tensor'), parts along dimension 0
The draws below stay inside these ranges and needn't reach their ends.
There are 2 independent parts, one for each index of `groups`. The reference program is written for one: setup_inputs(seed, part) draws one part's arguments, and reference() takes and returns one part's arrays. A program takes and returns all parts, laid end to end along the dimension named above; an argument that names none is the same for every part. Nothing has to cross between parts.
Inputs may be any that keep to these rules, and one draw needn't show every extreme that they name: `route_ids`: the two ids of a token differ. Within the 256 tokens of one image no expert is named more than 2 * 128 times; in some image some expert is named exactly 2 * 128 times. partner is a permutation of the experts with partner[e] != e for every e.
All inputs are finite; a program needn't handle non-finite values.
Results may differ from the reference program's by a relative error of at most 0.014.
Values may be sent and summed in bfloat16 or wider, within the bound.
A program may use at most 64 MiB of HBM per device.

```python
import math
import jax
import jax.numpy as jnp
import numpy as np
from jax import lax

D = 2048
FF = 4096
TOK_DEV = 256
EXPERTS = 4
IMAGES = 4
TOKENS = 1024
CAP = 128
N_TENSOR = 4


def draw_partner(key, part):
    order = jax.random.permutation(key, EXPERTS).astype(jnp.int32)
    following = jnp.roll(order, -1)
    return jnp.zeros((EXPERTS,), jnp.int32).at[order].set(following).astype(jnp.int32)


def shard_levels(rng, extent, shards, low, largest):
    level = 1.0
    for axis_at, shards_of in shards:
        heights = jax.random.uniform(jax.random.fold_in(jax.random.fold_in(rng, 6), axis_at), (shards_of,), jnp.float32, low / len(shards), largest / len(shards))
        level = level * jnp.repeat(jnp.exp(heights), extent[axis_at] // shards_of).reshape((-1,) + (1,) * (len(extent) - 1 - axis_at))
    return level


def deal_out(stream_key, own, number, rows, count, top, bound, lean):
    sequence = jax.random.permutation(stream_key, count)
    crowded, ordinary = portions_of(count, rows * top, bound, lean, True), portions_of(count, rows * top, bound, lean, False)
    places = jnp.arange(count)

    def named(lengths, offset_by):
        used = int((lengths > 0).sum())
        fixed = max(1, used // 4)
        shifted = fixed + (places - fixed + offset_by * (used - fixed)) % max(1, count - fixed)
        return jnp.zeros((count,), jnp.int32).at[sequence[jnp.where(places < fixed, places, shifted)]].set(jnp.asarray(lengths, jnp.int32))

    lengths = jnp.where(number % 4 == 0, named(crowded, number // 4), named(ordinary, number - number // 4 - 1))
    mixed = jax.random.permutation(jax.random.fold_in(own, 3), count)
    giver, taker = mixed[0:count // 2 * 2:2], mixed[1:count // 2 * 2:2]
    slack = jnp.minimum(lengths[giver] - 1, bound - lengths[taker]) // 2
    slack = jnp.where((giver == sequence[0]) | (taker == sequence[0]) | (lengths[taker] == 0), 0, jnp.maximum(slack, 0))
    shifted = jax.random.randint(jax.random.fold_in(own, 4), (count // 2,), 0, 1 << 20) % (slack + 1)
    lengths = lengths.at[giver].add(-shifted).at[taker].add(shifted)
    labels = jnp.searchsorted(jnp.cumsum(lengths), jnp.arange(rows * top), side="right").astype(jnp.int32)
    grid = labels.reshape(top, rows).T
    grid = grid[jax.random.permutation(jax.random.fold_in(own, 1), rows)]
    offset_by = jax.random.randint(jax.random.fold_in(own, 2), (rows, 1), 0, top)
    return jnp.take_along_axis(grid, (jnp.arange(top)[None, :] + offset_by) % top, axis=1)


def portions_of(number_of, total, most, lean, full):
    loads = [(1 << 20) // math.isqrt(rank ** lean) + 1 for rank in range(1, number_of + 1)]
    largest = most if full else min(most, max(-(-total // number_of), total * loads[0] // sum(loads)))
    least = 1 if total - largest >= number_of - 1 else 0
    given, spare = [largest] + [least] * (number_of - 1), total - largest - least * (number_of - 1)
    while spare > 0:
        candidates = [i for i in range(1, number_of) if given[i] < largest] or [i for i in range(1, number_of) if given[i] < most]
        whole, left = sum([loads[i] for i in candidates]), spare
        for i in candidates:
            more = min(most - given[i], max(1, left * loads[i] // whole), spare)
            given[i] = given[i] + more
            spare = spare - more
    return np.array(given)


def normal_values(stream_key, shape, scale, most, cuts=(), kind=jnp.bfloat16):
    gain = shard_levels(stream_key, shape, cuts, -0.22, 0.18) if cuts else 1.0
    values = jax.random.normal(stream_key, shape, jnp.float32) * scale * gain
    return jnp.minimum(jnp.maximum(values, -most), most).astype(kind)


def setup_inputs(seed: int = 0, part: int = 0) -> dict:
    key_of = jax.random.split(jax.random.key(seed), 12)
    part_splits = jax.random.split(jax.random.fold_in(key_of[11], part), 12)
    tokens = normal_values(part_splits[0], (TOKENS, D), 1.0, 6.0, ((0, 4),))
    route_ids_keys = jax.random.split(jax.random.fold_in(part_splits[1], 1), TOKENS // TOK_DEV)
    route_ids_turns = jax.random.permutation(jax.random.fold_in(part_splits[1], 3), TOKENS // TOK_DEV)
    route_ids = jax.vmap(lambda own, number: deal_out(jax.random.fold_in(part_splits[1], 2), own, number, TOK_DEV, EXPERTS, 2, 2 * CAP, 2))(route_ids_keys, route_ids_turns).reshape((TOKENS, 2))
    route_weights = jnp.clip(0.2 + 0.8 * jax.random.uniform(part_splits[2], (TOKENS, 2), jnp.float32) ** shard_levels(part_splits[2], (TOKENS, 2), ((0, 4),), -0.2, 0.2), 0.2, 1.0)
    modulation = normal_values(part_splits[3], (IMAGES, 3 * D), 1.0, 5.0, ((0, 4),), jnp.float32)
    partner = draw_partner(jax.random.fold_in(key_of[11], 71), part)
    w_gate = normal_values(key_of[5], (EXPERTS, D, FF), D ** -0.5, 0.125, ((0, 4), (2, 4)))
    w_up = normal_values(key_of[6], (EXPERTS, D, FF), D ** -0.5, 0.125, ((0, 4), (2, 4)))
    w_down = normal_values(key_of[7], (EXPERTS, FF, D), FF ** -0.5, 0.09375, ((0, 4), (1, 4)))
    spare_gate = normal_values(key_of[8], (EXPERTS, D, FF), D ** -0.5, 0.125, ((0, 4), (2, 4)))
    spare_up = normal_values(key_of[9], (EXPERTS, D, FF), D ** -0.5, 0.125, ((0, 4), (2, 4)))
    spare_down = normal_values(key_of[10], (EXPERTS, FF, D), FF ** -0.5, 0.09375, ((0, 4), (1, 4)))
    return dict(tokens=tokens, route_ids=route_ids, route_weights=route_weights, modulation=modulation, partner=partner, w_gate=w_gate, w_up=w_up, w_down=w_down, spare_gate=spare_gate, spare_up=spare_up, spare_down=spare_down)


def slot_targets(ids, partner):
    flat = ids.reshape(-1).astype(jnp.int32)
    onehot = (flat[:, None] == jnp.arange(EXPERTS, dtype=jnp.int32)[None, :]).astype(jnp.int32)
    ranks = lax.optimization_barrier(jnp.sum((jnp.cumsum(onehot, axis=0) - 1) * onehot, axis=1)).astype(jnp.int32)
    spare_of = lax.optimization_barrier(jnp.sum(onehot * partner[None, :].astype(jnp.int32), axis=1)).astype(jnp.int32)
    server = jnp.where(ranks >= CAP, spare_of, flat).astype(jnp.int32)
    return (server * (2 * CAP) + ranks).astype(jnp.int32)

def modulate(block, mod_row):
    values = block.astype(jnp.float32)
    mean = lax.optimization_barrier(jnp.mean(values, axis=1, keepdims=True))
    centred = values - mean
    var = lax.optimization_barrier(jnp.mean(centred * centred, axis=1, keepdims=True))
    normed = centred / jnp.sqrt(var + 1e-06)
    return (normed * (1.0 + mod_row[D:2 * D]) + mod_row[0:D]).astype(jnp.bfloat16)

def expert_apply(rows, gate_w, up_w, down_w):
    width = FF // N_TENSOR
    total = jnp.zeros((rows.shape[0], D), jnp.float32)
    for shard in range(N_TENSOR):
        lower = shard * width
        gate = jnp.dot(rows, gate_w[:, lower:lower + width], preferred_element_type=jnp.float32)
        upper = jnp.dot(rows, up_w[:, lower:lower + width], preferred_element_type=jnp.float32)
        hidden = (jax.nn.silu(gate) * upper).astype(jnp.bfloat16)
        piece = jnp.dot(hidden, down_w[lower:lower + width, :], preferred_element_type=jnp.float32).astype(jnp.bfloat16)
        piece = lax.optimization_barrier(piece)
        total = total + piece.astype(jnp.float32)
    return total

def device_apply(operands):
    block, gate_w, up_w, down_w, gate_s, up_s, down_s = operands
    home = expert_apply(block[:, 0].reshape(IMAGES * CAP, D), gate_w, up_w, down_w)
    spare = expert_apply(block[:, 1].reshape(IMAGES * CAP, D), gate_s, up_s, down_s)
    return jnp.stack((home.reshape(IMAGES, CAP, D), spare.reshape(IMAGES, CAP, D)), axis=1)

def reference(tokens, route_ids, route_weights, modulation, partner, w_gate, w_up, w_down, spare_gate, spare_up, spare_down):
    blocks = tokens.reshape(IMAGES, TOK_DEV, D)
    modded = jax.vmap(modulate)(blocks, modulation)
    targets = jax.vmap(slot_targets, in_axes=(0, None))(route_ids.reshape(IMAGES, TOK_DEV, 2), partner)

    def fill(rows, target):
        spread = jnp.repeat(rows, 2, axis=0)
        return jnp.zeros((EXPERTS * 2 * CAP, D), jnp.bfloat16).at[target].set(spread)
    sent = jax.vmap(fill)(modded, targets).reshape(IMAGES, EXPERTS, 2, CAP, D)
    arrived = jnp.transpose(sent, (1, 0, 2, 3, 4))
    outputs = lax.map(device_apply, (arrived, w_gate, w_up, w_down, spare_gate, spare_up, spare_down))
    outputs = jnp.transpose(outputs, (1, 0, 2, 3, 4)).reshape(IMAGES, EXPERTS * 2 * CAP, D)

    def finish(block, result, target, weights, mod_row):
        picked = result[target].reshape(TOK_DEV, 2, D)
        mixed = lax.optimization_barrier(jnp.sum(picked * weights[:, :, None], axis=1))
        return (block.astype(jnp.float32) + mod_row[2 * D:3 * D] * mixed).astype(jnp.bfloat16)
    final = jax.vmap(finish)(blocks, outputs, targets, route_weights.reshape(IMAGES, TOK_DEV, 2), modulation)
    return final.reshape(TOKENS, D)
```

```python
import jax
import jax.numpy as jnp
from jax import lax
from jax.sharding import PartitionSpec as P


CHUNKS = 2


def dot32(a, b):
    return jnp.dot(a, b, preferred_element_type=jnp.float32)


def pair_targets(ids, partner, experts, capacity):
    rows = ids.shape[0]
    onehot = (ids[:, :, None] == jnp.arange(experts, dtype=jnp.int32)).astype(jnp.float32)
    named = (onehot[:, 0] + onehot[:, 1]).astype(jnp.bfloat16)
    order = jnp.arange(rows, dtype=jnp.int32)
    before = (order[:, None] > order[None, :]).astype(jnp.bfloat16)
    earlier = dot32(before, named)
    ranks = jnp.sum(onehot * earlier[:, None, :], axis=2).astype(jnp.int32)
    spare_of = jnp.sum(onehot * partner.astype(jnp.float32), axis=2).astype(jnp.int32)
    server = jnp.where(ranks >= capacity, spare_of, ids)
    return server * (2 * capacity) + ranks


def modulate(values, mod_row, width):
    mean = jnp.mean(values, axis=1, keepdims=True)
    centred = values - mean
    var = jnp.mean(centred * centred, axis=1, keepdims=True)
    normed = centred / jnp.sqrt(var + 1e-06)
    return (normed * (1.0 + mod_row[width : 2 * width]) + mod_row[0:width]).astype(jnp.bfloat16)


def hidden_of(rows, gate, up):
    return (jax.nn.silu(dot32(rows, gate)) * dot32(rows, up)).astype(jnp.bfloat16)


def by_tokens(modded, targets, weights, capacity, experts, shards, sets):
    rows, width = modded.shape
    columns = width // shards
    slots = 2 * capacity
    me = lax.axis_index("expert")
    packed = jnp.concatenate((targets.astype(jnp.float32), weights), axis=1).T
    routes = lax.all_gather(packed, "expert")
    seen = lax.all_gather(modded, "expert")
    local = routes[:, 0:2].astype(jnp.int32) - me * slots
    number = jnp.arange(slots, dtype=jnp.int32)[None, :, None]
    hits = [local[:, j][:, None, :] == number for j in range(2)]
    pick = (hits[0] | hits[1]).astype(jnp.bfloat16)
    factor = sum(
        jnp.sum(jnp.where(hits[j], routes[:, 2 + j][:, None, :], 0.0), axis=2) for j in range(2)
    )
    hidden = []
    for which, (gate, up, _) in enumerate(sets):
        part = slice(which * capacity, (which + 1) * capacity)
        arrived = lax.dot_general(
            pick[:, part], seen, (((2,), (1,)), ((0,), (0,))), preferred_element_type=jnp.float32
        ).astype(jnp.bfloat16)
        hidden.append(hidden_of(arrived.reshape(experts * capacity, width), gate, up))
    sums = []
    step = columns // CHUNKS
    for c in range(CHUNKS):
        done = []
        for which, (_, _, down) in enumerate(sets):
            piece = down.reshape(-1, shards, columns)[:, :, c * step : (c + 1) * step]
            out = dot32(hidden[which], piece.reshape(-1, shards * step))
            out = out.reshape(experts, capacity, shards * step)
            scale = factor[:, which * capacity : (which + 1) * capacity]
            done.append((out * scale[:, :, None]).astype(jnp.bfloat16))
        served = jnp.concatenate(done, axis=1)
        part = lax.dot_general(
            pick, served, (((1,), (1,)), ((0,), (0,))), preferred_element_type=jnp.float32
        ).astype(jnp.bfloat16)
        own = lax.psum_scatter(
            part.reshape(experts * rows, shards * step), "expert", scatter_dimension=0, tiled=True
        )
        sums.append(lax.psum_scatter(own, "tensor", scatter_dimension=1, tiled=True))
    return jnp.concatenate(sums, axis=1).astype(jnp.float32)


def by_slots(modded, targets, weights, capacity, experts, shards, sets):
    rows, width = modded.shape
    columns = width // shards
    slots = experts * 2 * capacity
    number = jnp.arange(slots, dtype=jnp.int32)
    hits = [targets[:, j][:, None] == number[None, :] for j in range(2)]
    pick = (hits[0] | hits[1]).astype(jnp.bfloat16)
    outgoing = lax.dot_general(
        pick, modded, (((0,), (0,)), ((), ())), preferred_element_type=jnp.float32
    ).astype(jnp.bfloat16)
    outgoing = outgoing.reshape(experts, 2, capacity, width)
    back = []
    for which, (gate, up, down) in enumerate(sets):
        arrived = lax.all_to_all(
            outgoing[:, which], "expert", split_axis=0, concat_axis=0, tiled=True
        ).reshape(experts * capacity, width)
        part = dot32(hidden_of(arrived, gate, up), down).astype(jnp.bfloat16)
        shares = lax.psum_scatter(part, "tensor", scatter_dimension=1, tiled=True)
        back.append(
            lax.all_to_all(
                shares.reshape(experts, capacity, columns),
                "expert",
                split_axis=0,
                concat_axis=0,
                tiled=True,
            )
        )
    flat = jnp.stack(back, axis=1).reshape(slots, columns)
    return sum(
        dot32(hits[j].astype(jnp.bfloat16), flat) * weights[:, j : j + 1] for j in range(2)
    )


def per_device(
    tokens,
    route_ids,
    route_weights,
    modulation,
    partner,
    w_gate,
    w_up,
    w_down,
    spare_gate,
    spare_up,
    spare_down,
):
    experts = lax.axis_size("expert")
    shards = lax.axis_size("tensor")
    rows, width = tokens.shape
    capacity = 2 * rows // experts
    columns = width // shards
    mod_row = modulation[0]
    tensor_start = lax.axis_index("tensor") * columns
    modded = modulate(tokens.astype(jnp.float32), mod_row, width)
    targets = pair_targets(route_ids, partner, experts, capacity)
    sets = ((w_gate[0], w_up[0], w_down[0]), (spare_gate[0], spare_up[0], spare_down[0]))
    plan = by_tokens if 2 * capacity >= rows else by_slots
    mixed = plan(modded, targets, route_weights, capacity, experts, shards, sets)
    own_cols = lax.dynamic_slice_in_dim(tokens, tensor_start, columns, 1).astype(jnp.float32)
    gate_cols = lax.dynamic_slice_in_dim(mod_row, 2 * width + tensor_start, columns, 0)
    return (own_cols + gate_cols[None, :] * mixed).astype(jnp.bfloat16)


def solution(mesh):
    placed = (
        P(("groups", "expert"), None),
        P(("groups", "expert"), None),
        P(("groups", "expert"), None),
        P(("groups", "expert"), None),
        P(),
        P("expert", None, "tensor"),
        P("expert", None, "tensor"),
        P("expert", "tensor", None),
        P("expert", None, "tensor"),
        P("expert", None, "tensor"),
        P("expert", "tensor", None),
    )
    return jax.shard_map(
        per_device,
        mesh=mesh,
        in_specs=placed,
        out_specs=P(("groups", "expert"), "tensor"),
        check_vma=False,
    )
```

```python
import jax
import jax.numpy as jnp
from jax import lax
from jax.sharding import PartitionSpec as P


CHUNKS = 2


def dot32(a, b):
    return jnp.dot(a, b, preferred_element_type=jnp.float32)


def pair_targets(ids, partner, experts, capacity):
    rows = ids.shape[0]
    onehot = (ids[:, :, None] == jnp.arange(experts, dtype=jnp.int32)).astype(jnp.float32)
    named = (onehot[:, 0] + onehot[:, 1]).astype(jnp.bfloat16)
    order = jnp.arange(rows, dtype=jnp.int32)
    before = (order[:, None] > order[None, :]).astype(jnp.bfloat16)
    earlier = dot32(before, named)
    ranks = jnp.sum(onehot * earlier[:, None, :], axis=2).astype(jnp.int32)
    spare_of = jnp.sum(onehot * partner.astype(jnp.float32), axis=2).astype(jnp.int32)
    server = jnp.where(ranks >= capacity, spare_of, ids)
    return server * (2 * capacity) + ranks


def modulate(values, mod_row, width):
    mean = jnp.mean(values, axis=1, keepdims=True)
    centred = values - mean
    var = jnp.mean(centred * centred, axis=1, keepdims=True)
    normed = centred / jnp.sqrt(var + 1e-06)
    return (normed * (1.0 + mod_row[width : 2 * width]) + mod_row[0:width]).astype(jnp.bfloat16)


def hidden_of(rows, gate, up):
    return (jax.nn.silu(dot32(rows, gate)) * dot32(rows, up)).astype(jnp.bfloat16)


def swap(value, axis, bit):
    count = lax.axis_size(axis)
    return lax.ppermute(value, axis, [(i, i ^ bit) for i in range(count)])


def gather_near(value, axis):
    blocks = {0: value}
    bit = lax.axis_size(axis) // 2
    while bit:
        blocks.update({r ^ bit: swap(v, axis, bit) for r, v in list(blocks.items())})
        bit //= 2
    return blocks


def reduce_near(blocks, axis):
    bit, count = 1, lax.axis_size(axis)
    while bit < count:
        sent = {r: swap(v.astype(jnp.bfloat16), axis, bit) for r, v in blocks.items() if r & bit}
        blocks = {r: v + sent[r | bit].astype(jnp.float32) for r, v in blocks.items() if not r & bit}
        bit *= 2
    return blocks[0]


def by_tokens(modded, targets, weights, capacity, experts, shards, sets):
    rows, width = modded.shape
    columns = width // shards
    slots = 2 * capacity
    me = lax.axis_index("expert")
    mine = lax.axis_index("tensor")
    packed = jnp.concatenate((targets.astype(jnp.float32), weights), axis=1).T
    routes = gather_near(packed, "expert")
    seen = gather_near(modded, "expert")
    number = jnp.arange(slots, dtype=jnp.int32)[:, None]
    pick, factor = {}, {}
    for r, route in routes.items():
        local = route[0:2].astype(jnp.int32) - me * slots
        hits = [local[j][None, :] == number for j in range(2)]
        pick[r] = (hits[0] | hits[1]).astype(jnp.bfloat16)
        factor[r] = sum(
            jnp.sum(jnp.where(hits[j], route[2 + j][None, :], 0.0), axis=1, keepdims=True)
            for j in range(2)
        )
    order = sorted(seen)
    served = {r: [] for r in order}
    for which, (gate, up, down) in enumerate(sets):
        part = slice(which * capacity, (which + 1) * capacity)
        arrived = [dot32(pick[r][part], seen[r]).astype(jnp.bfloat16) for r in order]
        hidden = hidden_of(jnp.concatenate(arrived, axis=0), gate, up)
        scale = jnp.concatenate([factor[r][part] for r in order], axis=0)
        out = (dot32(hidden, down) * scale).astype(jnp.bfloat16)
        for at, r in enumerate(order):
            served[r].append(out[at * capacity : (at + 1) * capacity])
    served = {r: jnp.concatenate(v, axis=0) for r, v in served.items()}
    sums = []
    step = rows // CHUNKS
    for c in range(CHUNKS):
        terms = {
            r: lax.dot_general(
                pick[r][:, c * step : (c + 1) * step],
                served[r],
                (((0,), (0,)), ((), ())),
                preferred_element_type=jnp.float32,
            )
            for r in order
        }
        own = reduce_near(terms, "expert")
        split = {
            r: lax.dynamic_slice_in_dim(own, (mine ^ r) * columns, columns, 1)
            for r in range(shards)
        }
        sums.append(reduce_near(split, "tensor"))
    return jnp.concatenate(sums, axis=0)


def by_slots(modded, targets, weights, capacity, experts, shards, sets):
    rows, width = modded.shape
    columns = width // shards
    slots = experts * 2 * capacity
    number = jnp.arange(slots, dtype=jnp.int32)
    hits = [targets[:, j][:, None] == number[None, :] for j in range(2)]
    pick = (hits[0] | hits[1]).astype(jnp.bfloat16)
    outgoing = lax.dot_general(
        pick, modded, (((0,), (0,)), ((), ())), preferred_element_type=jnp.float32
    ).astype(jnp.bfloat16)
    outgoing = outgoing.reshape(experts, 2, capacity, width)
    back = []
    for which, (gate, up, down) in enumerate(sets):
        arrived = lax.all_to_all(
            outgoing[:, which], "expert", split_axis=0, concat_axis=0, tiled=True
        ).reshape(experts * capacity, width)
        part = dot32(hidden_of(arrived, gate, up), down).astype(jnp.bfloat16)
        shares = lax.psum_scatter(part, "tensor", scatter_dimension=1, tiled=True)
        back.append(
            lax.all_to_all(
                shares.reshape(experts, capacity, columns),
                "expert",
                split_axis=0,
                concat_axis=0,
                tiled=True,
            )
        )
    flat = jnp.stack(back, axis=1).reshape(slots, columns)
    return sum(
        dot32(hits[j].astype(jnp.bfloat16), flat) * weights[:, j : j + 1] for j in range(2)
    )


def per_device(
    tokens,
    route_ids,
    route_weights,
    modulation,
    partner,
    w_gate,
    w_up,
    w_down,
    spare_gate,
    spare_up,
    spare_down,
):
    experts = lax.axis_size("expert")
    shards = lax.axis_size("tensor")
    rows, width = tokens.shape
    capacity = 2 * rows // experts
    columns = width // shards
    mod_row = modulation[0]
    tensor_start = lax.axis_index("tensor") * columns
    modded = modulate(tokens.astype(jnp.float32), mod_row, width)
    targets = pair_targets(route_ids, partner, experts, capacity)
    sets = ((w_gate[0], w_up[0], w_down[0]), (spare_gate[0], spare_up[0], spare_down[0]))
    paired = experts & (experts - 1) == 0 and shards & (shards - 1) == 0
    plan = by_tokens if paired and 2 * capacity >= rows else by_slots
    mixed = plan(modded, targets, route_weights, capacity, experts, shards, sets)
    own_cols = lax.dynamic_slice_in_dim(tokens, tensor_start, columns, 1).astype(jnp.float32)
    gate_cols = lax.dynamic_slice_in_dim(mod_row, 2 * width + tensor_start, columns, 0)
    return (own_cols + gate_cols[None, :] * mixed).astype(jnp.bfloat16)


def solution(mesh):
    placed = (
        P(("groups", "expert"), None),
        P(("groups", "expert"), None),
        P(("groups", "expert"), None),
        P(("groups", "expert"), None),
        P(),
        P("expert", None, "tensor"),
        P("expert", None, "tensor"),
        P("expert", "tensor", None),
        P("expert", None, "tensor"),
        P("expert", None, "tensor"),
        P("expert", "tensor", None),
    )
    return jax.shard_map(
        per_device,
        mesh=mesh,
        in_specs=placed,
        out_specs=P(("groups", "expert"), "tensor"),
        check_vma=False,
    )
```

```python
import jax
import jax.numpy as jnp
from jax import lax
from jax.sharding import PartitionSpec as P


CHUNKS = 2


def dot32(a, b):
    return jnp.dot(a, b, preferred_element_type=jnp.float32)


def pair_targets(ids, partner, experts, capacity):
    rows = ids.shape[0]
    onehot = (ids[:, :, None] == jnp.arange(experts, dtype=jnp.int32)).astype(jnp.float32)
    named = (onehot[:, 0] + onehot[:, 1]).astype(jnp.bfloat16)
    order = jnp.arange(rows, dtype=jnp.int32)
    before = (order[:, None] > order[None, :]).astype(jnp.bfloat16)
    earlier = dot32(before, named)
    ranks = jnp.sum(onehot * earlier[:, None, :], axis=2).astype(jnp.int32)
    spare_of = jnp.sum(onehot * partner.astype(jnp.float32), axis=2).astype(jnp.int32)
    server = jnp.where(ranks >= capacity, spare_of, ids)
    return server * (2 * capacity) + ranks


def modulate(values, mod_row, width):
    mean = jnp.mean(values, axis=1, keepdims=True)
    centred = values - mean
    var = jnp.mean(centred * centred, axis=1, keepdims=True)
    normed = centred / jnp.sqrt(var + 1e-06)
    return (normed * (1.0 + mod_row[width : 2 * width]) + mod_row[0:width]).astype(jnp.bfloat16)


def hidden_of(rows, gate, up):
    gated, raised = lax.optimization_barrier((dot32(rows, gate), dot32(rows, up)))
    return (jax.nn.silu(gated) * raised).astype(jnp.bfloat16)


def swap(value, axis, bit):
    count = lax.axis_size(axis)
    return lax.ppermute(value, axis, [(i, i ^ bit) for i in range(count)])


def gather_near(value, axis):
    blocks = {0: value}
    bit = lax.axis_size(axis) // 2
    while bit:
        blocks.update({r ^ bit: swap(v, axis, bit) for r, v in list(blocks.items())})
        bit //= 2
    return blocks


def reduce_near(blocks, axis):
    bit, count = 1, lax.axis_size(axis)
    while bit < count:
        sent = {r: swap(v.astype(jnp.bfloat16), axis, bit) for r, v in blocks.items() if r & bit}
        blocks = {r: v + sent[r | bit].astype(jnp.float32) for r, v in blocks.items() if not r & bit}
        bit *= 2
    return blocks[0]


def by_tokens(modded, targets, weights, capacity, experts, shards, sets):
    rows, width = modded.shape
    columns = width // shards
    slots = 2 * capacity
    me = lax.axis_index("expert")
    mine = lax.axis_index("tensor")
    packed = jnp.concatenate((targets.astype(jnp.float32), weights), axis=1).T
    routes = gather_near(packed, "expert")
    seen = gather_near(modded, "expert")
    number = jnp.arange(slots, dtype=jnp.int32)[:, None]
    pick, factor = {}, {}
    for r, route in routes.items():
        local = route[0:2].astype(jnp.int32) - me * slots
        hits = [local[j][None, :] == number for j in range(2)]
        pick[r] = (hits[0] | hits[1]).astype(jnp.bfloat16)
        factor[r] = sum(
            jnp.sum(jnp.where(hits[j], route[2 + j][None, :], 0.0), axis=1, keepdims=True)
            for j in range(2)
        )
    order = sorted(seen)
    served = {r: [] for r in order}
    near = max(1, experts // 2)
    for group in (order[:near], order[near:]):
        for which, (gate, up, down) in enumerate(sets if group else ()):
            part = slice(which * capacity, (which + 1) * capacity)
            arrived = [dot32(pick[r][part], seen[r]).astype(jnp.bfloat16) for r in group]
            hidden = hidden_of(jnp.concatenate(arrived, axis=0), gate, up)
            scale = jnp.concatenate([factor[r][part] for r in group], axis=0)
            out = (dot32(hidden, down) * scale).astype(jnp.bfloat16)
            for at, r in enumerate(group):
                served[r].append(out[at * capacity : (at + 1) * capacity])
    served = {r: jnp.concatenate(v, axis=0) for r, v in served.items()}
    sums = []
    step = rows // CHUNKS
    for c in range(CHUNKS):
        terms = {
            r: lax.dot_general(
                pick[r][:, c * step : (c + 1) * step],
                served[r],
                (((0,), (0,)), ((), ())),
                preferred_element_type=jnp.float32,
            )
            for r in order
        }
        own = reduce_near(terms, "expert")
        split = {
            r: lax.dynamic_slice_in_dim(own, (mine ^ r) * columns, columns, 1)
            for r in range(shards)
        }
        sums.append(reduce_near(split, "tensor"))
    return jnp.concatenate(sums, axis=0)


def by_slots(modded, targets, weights, capacity, experts, shards, sets):
    rows, width = modded.shape
    columns = width // shards
    slots = experts * 2 * capacity
    number = jnp.arange(slots, dtype=jnp.int32)
    hits = [targets[:, j][:, None] == number[None, :] for j in range(2)]
    pick = (hits[0] | hits[1]).astype(jnp.bfloat16)
    outgoing = lax.dot_general(
        pick, modded, (((0,), (0,)), ((), ())), preferred_element_type=jnp.float32
    ).astype(jnp.bfloat16)
    outgoing = outgoing.reshape(experts, 2, capacity, width)
    back = []
    for which, (gate, up, down) in enumerate(sets):
        arrived = lax.all_to_all(
            outgoing[:, which], "expert", split_axis=0, concat_axis=0, tiled=True
        ).reshape(experts * capacity, width)
        part = dot32(hidden_of(arrived, gate, up), down).astype(jnp.bfloat16)
        shares = lax.psum_scatter(part, "tensor", scatter_dimension=1, tiled=True)
        back.append(
            lax.all_to_all(
                shares.reshape(experts, capacity, columns),
                "expert",
                split_axis=0,
                concat_axis=0,
                tiled=True,
            )
        )
    flat = jnp.stack(back, axis=1).reshape(slots, columns)
    return sum(
        dot32(hits[j].astype(jnp.bfloat16), flat) * weights[:, j : j + 1] for j in range(2)
    )


def per_device(
    tokens,
    route_ids,
    route_weights,
    modulation,
    partner,
    w_gate,
    w_up,
    w_down,
    spare_gate,
    spare_up,
    spare_down,
):
    experts = lax.axis_size("expert")
    shards = lax.axis_size("tensor")
    rows, width = tokens.shape
    capacity = 2 * rows // experts
    columns = width // shards
    mod_row = modulation[0]
    tensor_start = lax.axis_index("tensor") * columns
    modded = modulate(tokens.astype(jnp.float32), mod_row, width)
    targets = pair_targets(route_ids, partner, experts, capacity)
    sets = ((w_gate[0], w_up[0], w_down[0]), (spare_gate[0], spare_up[0], spare_down[0]))
    paired = experts & (experts - 1) == 0 and shards & (shards - 1) == 0
    plan = by_tokens if paired and 2 * capacity >= rows else by_slots
    mixed = plan(modded, targets, route_weights, capacity, experts, shards, sets)
    own_cols = lax.dynamic_slice_in_dim(tokens, tensor_start, columns, 1).astype(jnp.float32)
    gate_cols = lax.dynamic_slice_in_dim(mod_row, 2 * width + tensor_start, columns, 0)
    return (own_cols + gate_cols[None, :] * mixed).astype(jnp.bfloat16)


def solution(mesh):
    placed = (
        P(("groups", "expert"), None),
        P(("groups", "expert"), None),
        P(("groups", "expert"), None),
        P(("groups", "expert"), None),
        P(),
        P("expert", None, "tensor"),
        P("expert", None, "tensor"),
        P("expert", "tensor", None),
        P("expert", None, "tensor"),
        P("expert", None, "tensor"),
        P("expert", "tensor", None),
    )
    return jax.shard_map(
        per_device,
        mesh=mesh,
        in_specs=placed,
        out_specs=P(("groups", "expert"), "tensor"),
        check_vma=False,
    )
```

```python
import jax
import jax.numpy as jnp
from jax import lax
from jax.sharding import PartitionSpec as P


def dot32(a, b):
    return jnp.dot(a, b, preferred_element_type=jnp.float32)


def pair_targets(ids, partner, experts, capacity):
    rows = ids.shape[0]
    onehot = (ids[:, :, None] == jnp.arange(experts, dtype=jnp.int32)).astype(jnp.float32)
    named = (onehot[:, 0] + onehot[:, 1]).astype(jnp.bfloat16)
    order = jnp.arange(rows, dtype=jnp.int32)
    before = (order[:, None] > order[None, :]).astype(jnp.bfloat16)
    earlier = dot32(before, named)
    ranks = jnp.sum(onehot * earlier[:, None, :], axis=2).astype(jnp.int32)
    spare_of = jnp.sum(onehot * partner.astype(jnp.float32), axis=2).astype(jnp.int32)
    server = jnp.where(ranks >= capacity, spare_of, ids)
    return server * (2 * capacity) + ranks


def modulate(values, mod_row, width):
    mean = jnp.mean(values, axis=1, keepdims=True)
    centred = values - mean
    var = jnp.mean(centred * centred, axis=1, keepdims=True)
    normed = centred / jnp.sqrt(var + 1e-06)
    return (normed * (1.0 + mod_row[width : 2 * width]) + mod_row[0:width]).astype(jnp.bfloat16)


def hidden_of(rows, gate, up):
    gated, raised = lax.optimization_barrier((dot32(rows, gate), dot32(rows, up)))
    return (jax.nn.silu(gated) * raised).astype(jnp.bfloat16)


def swap(value, axis, bit):
    count = lax.axis_size(axis)
    return lax.ppermute(value, axis, [(i, i ^ bit) for i in range(count)])


def gather_near(value, axis):
    blocks = {0: value}
    bit = lax.axis_size(axis) // 2
    while bit:
        blocks.update({r ^ bit: swap(v, axis, bit) for r, v in list(blocks.items())})
        bit //= 2
    return blocks


def bits_of(axis):
    return [1 << k for k in range(lax.axis_size(axis).bit_length() - 1)]


def reduce_near(blocks, axis, bits):
    for bit in bits:
        sent = {r: swap(v.astype(jnp.bfloat16), axis, bit) for r, v in blocks.items() if r & bit}
        blocks = {r: v + sent[r | bit].astype(jnp.float32) for r, v in blocks.items() if not r & bit}
    return blocks


def by_tokens(modded, targets, weights, capacity, experts, shards, sets):
    rows, width = modded.shape
    columns = width // shards
    slots = 2 * capacity
    me = lax.axis_index("expert")
    mine = lax.axis_index("tensor")
    packed = jnp.concatenate((targets.astype(jnp.float32), weights), axis=1).T
    routes = gather_near(packed, "expert")
    seen = gather_near(modded, "expert")
    number = jnp.arange(slots, dtype=jnp.int32)[:, None]
    pick, factor = {}, {}
    for r, route in routes.items():
        local = route[0:2].astype(jnp.int32) - me * slots
        hits = [local[j][None, :] == number for j in range(2)]
        pick[r] = (hits[0] | hits[1]).astype(jnp.bfloat16)
        factor[r] = sum(
            jnp.sum(jnp.where(hits[j], route[2 + j][None, :], 0.0), axis=1, keepdims=True)
            for j in range(2)
        )
    order = sorted(seen)
    served = {r: [] for r in order}
    near = max(1, experts // 2)
    for group in (order[:near], order[near:]):
        for which, (gate, up, down) in enumerate(sets if group else ()):
            part = slice(which * capacity, (which + 1) * capacity)
            arrived = [dot32(pick[r][part], seen[r]).astype(jnp.bfloat16) for r in group]
            hidden = hidden_of(jnp.concatenate(arrived, axis=0), gate, up)
            scale = jnp.concatenate([factor[r][part] for r in group], axis=0)
            out = (dot32(hidden, down) * scale).astype(jnp.bfloat16)
            for at, r in enumerate(group):
                served[r].append(out[at * capacity : (at + 1) * capacity])
    served = {r: jnp.concatenate(v, axis=0) for r, v in served.items()}
    def columns_of(term):
        split = {
            r: lax.dynamic_slice_in_dim(term, (mine ^ r) * columns, columns, 1)
            for r in range(shards)
        }
        return reduce_near(split, "tensor", bits_of("tensor"))[0]

    close, far = bits_of("expert")[:1], bits_of("expert")[1:]
    cut = rows * 5 // 8 // 16 * 16
    sums = []
    for lower, upper in ((0, cut), (cut, rows)):
        terms = {
            r: lax.dot_general(
                pick[r][:, lower:upper],
                served[r],
                (((0,), (0,)), ((), ())),
                preferred_element_type=jnp.float32,
            )
            for r in order
        }
        chip = reduce_near(terms, "expert", close)
        if lower == 0:
            sums.append(columns_of(reduce_near(chip, "expert", far)[0]))
        else:
            narrow = {r: columns_of(v) for r, v in chip.items()}
            sums.append(reduce_near(narrow, "expert", far)[0])
    return jnp.concatenate(sums, axis=0)


def by_slots(modded, targets, weights, capacity, experts, shards, sets):
    rows, width = modded.shape
    columns = width // shards
    slots = experts * 2 * capacity
    number = jnp.arange(slots, dtype=jnp.int32)
    hits = [targets[:, j][:, None] == number[None, :] for j in range(2)]
    pick = (hits[0] | hits[1]).astype(jnp.bfloat16)
    outgoing = lax.dot_general(
        pick, modded, (((0,), (0,)), ((), ())), preferred_element_type=jnp.float32
    ).astype(jnp.bfloat16)
    outgoing = outgoing.reshape(experts, 2, capacity, width)
    back = []
    for which, (gate, up, down) in enumerate(sets):
        arrived = lax.all_to_all(
            outgoing[:, which], "expert", split_axis=0, concat_axis=0, tiled=True
        ).reshape(experts * capacity, width)
        part = dot32(hidden_of(arrived, gate, up), down).astype(jnp.bfloat16)
        shares = lax.psum_scatter(part, "tensor", scatter_dimension=1, tiled=True)
        back.append(
            lax.all_to_all(
                shares.reshape(experts, capacity, columns),
                "expert",
                split_axis=0,
                concat_axis=0,
                tiled=True,
            )
        )
    flat = jnp.stack(back, axis=1).reshape(slots, columns)
    return sum(
        dot32(hits[j].astype(jnp.bfloat16), flat) * weights[:, j : j + 1] for j in range(2)
    )


def per_device(
    tokens,
    route_ids,
    route_weights,
    modulation,
    partner,
    w_gate,
    w_up,
    w_down,
    spare_gate,
    spare_up,
    spare_down,
):
    experts = lax.axis_size("expert")
    shards = lax.axis_size("tensor")
    rows, width = tokens.shape
    capacity = 2 * rows // experts
    columns = width // shards
    mod_row = modulation[0]
    tensor_start = lax.axis_index("tensor") * columns
    modded = modulate(tokens.astype(jnp.float32), mod_row, width)
    targets = pair_targets(route_ids, partner, experts, capacity)
    sets = ((w_gate[0], w_up[0], w_down[0]), (spare_gate[0], spare_up[0], spare_down[0]))
    paired = experts & (experts - 1) == 0 and shards & (shards - 1) == 0
    plan = by_tokens if paired and 2 * capacity >= rows else by_slots
    mixed = plan(modded, targets, route_weights, capacity, experts, shards, sets)
    own_cols = lax.dynamic_slice_in_dim(tokens, tensor_start, columns, 1).astype(jnp.float32)
    gate_cols = lax.dynamic_slice_in_dim(mod_row, 2 * width + tensor_start, columns, 0)
    return (own_cols + gate_cols[None, :] * mixed).astype(jnp.bfloat16)


def solution(mesh):
    placed = (
        P(("groups", "expert"), None),
        P(("groups", "expert"), None),
        P(("groups", "expert"), None),
        P(("groups", "expert"), None),
        P(),
        P("expert", None, "tensor"),
        P("expert", None, "tensor"),
        P("expert", "tensor", None),
        P("expert", None, "tensor"),
        P("expert", None, "tensor"),
        P("expert", "tensor", None),
    )
    return jax.shard_map(
        per_device,
        mesh=mesh,
        in_specs=placed,
        out_specs=P(("groups", "expert"), "tensor"),
        check_vma=False,
    )
```

```python
import jax
import jax.numpy as jnp
from jax import lax
from jax.sharding import PartitionSpec as P


def dot32(a, b):
    return jnp.dot(a, b, preferred_element_type=jnp.float32)


def pair_targets(ids, partner, experts, capacity):
    rows = ids.shape[1]
    names = jnp.arange(experts, dtype=jnp.int32)[:, None]
    onehot = [(ids[j][None, :] == names).astype(jnp.float32) for j in range(2)]
    order = jnp.arange(rows, dtype=jnp.int32)
    before = (order[:, None] < order[None, :]).astype(jnp.bfloat16)
    earlier = dot32((onehot[0] + onehot[1]).astype(jnp.bfloat16), before)
    spares = partner.astype(jnp.float32)[:, None]
    targets = []
    for j in range(2):
        rank = jnp.sum(onehot[j] * earlier, axis=0).astype(jnp.int32)
        spare_of = jnp.sum(onehot[j] * spares, axis=0).astype(jnp.int32)
        server = jnp.where(rank >= capacity, spare_of, ids[j])
        targets.append(server * (2 * capacity) + rank)
    return jnp.stack(targets)


def modulate(values, mod_row, width):
    mean = jnp.mean(values, axis=1, keepdims=True)
    centred = values - mean
    var = jnp.mean(centred * centred, axis=1, keepdims=True)
    normed = centred / jnp.sqrt(var + 1e-06)
    return (normed * (1.0 + mod_row[width : 2 * width]) + mod_row[0:width]).astype(jnp.bfloat16)


def hidden_of(rows, gate, up):
    gated, raised = lax.optimization_barrier((dot32(rows, gate), dot32(rows, up)))
    return (jax.nn.silu(gated) * raised).astype(jnp.bfloat16)


def swap(value, axis, bit):
    count = lax.axis_size(axis)
    return lax.ppermute(value, axis, [(i, i ^ bit) for i in range(count)])


def gather_near(value, axis):
    blocks = {0: value}
    bit = lax.axis_size(axis) // 2
    while bit:
        blocks.update({r ^ bit: swap(v, axis, bit) for r, v in list(blocks.items())})
        bit //= 2
    return blocks


def bits_of(axis):
    return [1 << k for k in range(lax.axis_size(axis).bit_length() - 1)]


def reduce_near(blocks, axis, bits):
    for bit in bits:
        sent = {r: swap(v.astype(jnp.bfloat16), axis, bit) for r, v in blocks.items() if r & bit}
        blocks = {r: v + sent[r | bit].astype(jnp.float32) for r, v in blocks.items() if not r & bit}
    return blocks


def by_tokens(modded, targets, weights, capacity, experts, shards, sets):
    rows, width = modded.shape
    columns = width // shards
    slots = 2 * capacity
    me = lax.axis_index("expert")
    mine = lax.axis_index("tensor")
    packed = jnp.concatenate((targets.astype(jnp.float32), weights.T), axis=0)
    routes = gather_near(packed, "expert")
    seen = gather_near(modded, "expert")
    number = jnp.arange(slots, dtype=jnp.int32)[:, None]
    pick, factor = {}, {}
    for r, route in routes.items():
        local = route[0:2].astype(jnp.int32) - me * slots
        hits = [local[j][None, :] == number for j in range(2)]
        pick[r] = (hits[0] | hits[1]).astype(jnp.bfloat16)
        factor[r] = sum(
            jnp.sum(jnp.where(hits[j], route[2 + j][None, :], 0.0), axis=1, keepdims=True)
            for j in range(2)
        )
    order = sorted(seen)
    served = {r: [] for r in order}
    near = max(1, experts // 2)
    for group in (order[:near], order[near:]):
        for which, (gate, up, down) in enumerate(sets if group else ()):
            part = slice(which * capacity, (which + 1) * capacity)
            arrived = [dot32(pick[r][part], seen[r]).astype(jnp.bfloat16) for r in group]
            hidden = hidden_of(jnp.concatenate(arrived, axis=0), gate, up)
            scale = jnp.concatenate([factor[r][part] for r in group], axis=0)
            out = (dot32(hidden, down) * scale).astype(jnp.bfloat16)
            for at, r in enumerate(group):
                served[r].append(out[at * capacity : (at + 1) * capacity])
    served = {r: jnp.concatenate(v, axis=0) for r, v in served.items()}
    def columns_of(term):
        split = {
            r: lax.dynamic_slice_in_dim(term, (mine ^ r) * columns, columns, 1)
            for r in range(shards)
        }
        return reduce_near(split, "tensor", bits_of("tensor"))[0]

    close, far = bits_of("expert")[:1], bits_of("expert")[1:]
    cut = rows * 5 // 8 // 16 * 16
    sums = []
    for lower, upper in ((0, cut), (cut, rows)):
        terms = {
            r: lax.dot_general(
                pick[r][:, lower:upper],
                served[r],
                (((0,), (0,)), ((), ())),
                preferred_element_type=jnp.float32,
            )
            for r in order
        }
        chip = reduce_near(terms, "expert", close)
        if lower == 0:
            sums.append(columns_of(reduce_near(chip, "expert", far)[0]))
        else:
            narrow = {r: columns_of(v) for r, v in chip.items()}
            sums.append(reduce_near(narrow, "expert", far)[0])
    return jnp.concatenate(sums, axis=0)


def by_slots(modded, targets, weights, capacity, experts, shards, sets):
    rows, width = modded.shape
    columns = width // shards
    slots = experts * 2 * capacity
    number = jnp.arange(slots, dtype=jnp.int32)
    hits = [targets[j][:, None] == number[None, :] for j in range(2)]
    pick = (hits[0] | hits[1]).astype(jnp.bfloat16)
    outgoing = lax.dot_general(
        pick, modded, (((0,), (0,)), ((), ())), preferred_element_type=jnp.float32
    ).astype(jnp.bfloat16)
    outgoing = outgoing.reshape(experts, 2, capacity, width)
    back = []
    for which, (gate, up, down) in enumerate(sets):
        arrived = lax.all_to_all(
            outgoing[:, which], "expert", split_axis=0, concat_axis=0, tiled=True
        ).reshape(experts * capacity, width)
        part = dot32(hidden_of(arrived, gate, up), down).astype(jnp.bfloat16)
        shares = lax.psum_scatter(part, "tensor", scatter_dimension=1, tiled=True)
        back.append(
            lax.all_to_all(
                shares.reshape(experts, capacity, columns),
                "expert",
                split_axis=0,
                concat_axis=0,
                tiled=True,
            )
        )
    flat = jnp.stack(back, axis=1).reshape(slots, columns)
    return sum(
        dot32(hits[j].astype(jnp.bfloat16), flat) * weights[:, j : j + 1] for j in range(2)
    )


def per_device(
    tokens,
    route_ids,
    route_weights,
    modulation,
    partner,
    w_gate,
    w_up,
    w_down,
    spare_gate,
    spare_up,
    spare_down,
):
    experts = lax.axis_size("expert")
    shards = lax.axis_size("tensor")
    rows, width = tokens.shape
    capacity = 2 * rows // experts
    columns = width // shards
    mod_row = modulation[0]
    tensor_start = lax.axis_index("tensor") * columns
    modded = modulate(tokens.astype(jnp.float32), mod_row, width)
    targets = pair_targets(route_ids.T, partner, experts, capacity)
    sets = ((w_gate[0], w_up[0], w_down[0]), (spare_gate[0], spare_up[0], spare_down[0]))
    paired = experts & (experts - 1) == 0 and shards & (shards - 1) == 0
    plan = by_tokens if paired and 2 * capacity >= rows else by_slots
    mixed = plan(modded, targets, route_weights, capacity, experts, shards, sets)
    own_cols = lax.dynamic_slice_in_dim(tokens, tensor_start, columns, 1).astype(jnp.float32)
    gate_cols = lax.dynamic_slice_in_dim(mod_row, 2 * width + tensor_start, columns, 0)
    return (own_cols + gate_cols[None, :] * mixed).astype(jnp.bfloat16)


def solution(mesh):
    placed = (
        P(("groups", "expert"), None),
        P(("groups", "expert"), None),
        P(("groups", "expert"), None),
        P(("groups", "expert"), None),
        P(),
        P("expert", None, "tensor"),
        P("expert", None, "tensor"),
        P("expert", "tensor", None),
        P("expert", None, "tensor"),
        P("expert", None, "tensor"),
        P("expert", "tensor", None),
    )
    return jax.shard_map(
        per_device,
        mesh=mesh,
        in_specs=placed,
        out_specs=P(("groups", "expert"), "tensor"),
        check_vma=False,
    )
```
